32 devices in a mesh: gx: 8 (over z, x), gy: 4 (over y, core).
Axes of the slice: x: 2, y: 2, z: 4, core: 2. Of those that a mesh axis runs over, the one named last changes fastest.
Arguments:
- parent_field: float32 [8, 1024, 2048], P(None, 'gx', 'gy'), may hold values from -6 to 6
- parent_sppt: bfloat16 [1024, 2048], P('gx', 'gy'), may hold values from -0.796875 to 0.796875
- child_storm: float32 [8, 1024, 1536], P(None, 'gx', 'gy'), may hold values from -6 to 6
- child_sppt: bfloat16 [1024, 1536], P('gx', 'gy'), may hold values from -0.796875 to 0.796875
- wind: float32 [2, 8], replicated, may hold values from -0.3 to 0.3
- strip_dest: int32 [1024, 1], replicated, may hold values from 0 to 31; in each aligned block of 32 rows (0 to 31, 32 to 63, ...) at most 2 rows name the same one
- strip_row: int32 [1024], replicated, may hold values from 0 to 511
- strip_target: int32 [1024], replicated, may hold values from 0 to 127
- storm_shift: int32 [2, 4], replicated, may hold values from 0 to 7, as said below
Outputs:
- new_parent: float32 [8, 1024, 2048], P(None, 'gx', 'gy')
- child: float32 [8, 1024, 1536], P(None, 'gx', 'gy')
The draws below stay inside these ranges and needn't reach their ends.
Inputs may be any that keep to these rules, and one draw needn't show every extreme that they name: `strip_dest`: among the 32 strips of one parent device no owner appears more than 2 times. `storm_shift`: row 0 lies in 0 to 8 - 1 and holds 8 - 1 at least once; row 1 lies in 0 to 4 - 1 and holds 4 - 1 at least once.
All inputs are finite; a program needn't handle non-finite values.
Results may differ from the reference program's by a relative error of at most 0.0003.
Values sent between devices are 32-bit elements; how exact they have to be, the bound alone decides.
A program may use at most 64 MiB of HBM per device.

```python
import math
import jax
import jax.numpy as jnp
import numpy as np
from jax import lax

LEV = 8
SUBSTEPS = 3
STRIP = 128
CAP = 2
NPIECE = 4
PBX = 128
PBY = 512
CROWS = 128
SLOTS = 32
PX = 32
CY = 384
NRB = 512
NPX = 1024
NPY = 2048
NCX = 1024
NCY = 1536
N_GX = 8
N_GY = 4
DEVICES = 32


def draw_storm_shift(key, part):
    keys = jax.random.split(key, 4)
    count_x = NCX // CROWS
    count_y = NCY // CY
    places = jnp.arange(NPIECE)
    shift_x = jax.random.randint(keys[0], (NPIECE,), 0, count_x)
    where_x = jax.random.randint(keys[1], (), 0, NPIECE)
    shift_x = jnp.where(places == where_x, count_x - 1, shift_x)
    shift_y = jax.random.randint(keys[2], (NPIECE,), 0, count_y)
    where_y = jax.random.randint(keys[3], (), 0, NPIECE)
    shift_y = jnp.where(places == where_y, count_y - 1, shift_y)
    return jnp.stack([shift_x, shift_y]).astype(jnp.int32)


def touch_ends(values, own_key, smallest, top_value):
    spot = [jax.random.randint(jax.random.fold_in(own_key, axis), (), 0, length) for axis, length in enumerate(values.shape)]
    main_axis = values.shape.index(max(values.shape))
    neighbour = spot[:main_axis] + [(spot[main_axis] + 1) % values.shape[main_axis]] + spot[main_axis + 1:]
    return values.at[tuple(spot)].set(smallest).at[tuple(neighbour)].set(top_value)


def levels(rng, shape, pieces, least, high):
    level, own = 1.0, jax.random.fold_in(rng, 6)
    for dim, shards_of in pieces:
        steps = jnp.exp(jax.random.uniform(jax.random.fold_in(own, dim), (shards_of,), jnp.float32, least / len(pieces), high / len(pieces)))
        level = level * jnp.repeat(steps, shape[dim] // shards_of).reshape([-1 if axis == dim else 1 for axis in range(len(shape))])
    return level


def deal_out(rng, own, number, rows, count, top, bound, lean):
    sequence = jax.random.permutation(rng, count)
    crowded, ordinary = shares(count, rows * top, bound, lean, True), shares(count, rows * top, bound, lean, False)
    places = jnp.arange(count)

    def named(lengths, turn):
        used = int((lengths > 0).sum())
        fixed = max(1, used // 4)
        passed = fixed + (places - fixed + turn * (used - fixed)) % max(1, count - fixed)
        return jnp.zeros((count,), jnp.int32).at[sequence[jnp.where(places < fixed, places, passed)]].set(jnp.asarray(lengths, jnp.int32))

    lengths = jnp.where(number % 4 == 0, named(crowded, number // 4), named(ordinary, number - number // 4 - 1))
    mixed = jax.random.permutation(jax.random.fold_in(own, 3), count)
    donor, receiver = mixed[0:count // 2 * 2:2], mixed[1:count // 2 * 2:2]
    slack = jnp.minimum(lengths[donor] - 1, bound - lengths[receiver]) // 2
    slack = jnp.where((donor == sequence[0]) | (receiver == sequence[0]) | (lengths[receiver] == 0), 0, jnp.maximum(slack, 0))
    passed = jax.random.randint(jax.random.fold_in(own, 4), (count // 2,), 0, 1 << 20) % (slack + 1)
    lengths = lengths.at[donor].add(-passed).at[receiver].add(passed)
    members = jnp.searchsorted(jnp.cumsum(lengths), jnp.arange(rows * top), side="right").astype(jnp.int32)
    grid = members.reshape(top, rows).T
    grid = grid[jax.random.permutation(jax.random.fold_in(own, 1), rows)]
    turn = jax.random.randint(jax.random.fold_in(own, 2), (rows, 1), 0, top)
    return jnp.take_along_axis(grid, (jnp.arange(top)[None, :] + turn) % top, axis=1)


def shares(amount, total, reach, slope, full):
    loads = [(1 << 20) // math.isqrt(standing ** slope) + 1 for standing in range(1, amount + 1)]
    largest = reach if full else min(reach, max(-(-total // amount), total * loads[0] // sum(loads)))
    least = 1 if total - largest >= amount - 1 else 0
    holding, spare = [largest] + [least] * (amount - 1), total - largest - least * (amount - 1)
    while spare > 0:
        movable = [i for i in range(1, amount) if holding[i] < largest] or [i for i in range(1, amount) if holding[i] < reach]
        mass, left = sum([loads[i] for i in movable]), spare
        for i in movable:
            addition = min(reach - holding[i], max(1, left * loads[i] // mass), spare)
            holding[i] = holding[i] + addition
            spare = spare - addition
    return np.array(holding)


def centred(own_key, dims, scale, most, cuts=(), kind=jnp.bfloat16):
    level = levels(own_key, dims, cuts, -0.22, 0.18) if cuts else 1.0
    result = jax.random.normal(own_key, dims, jnp.float32) * scale * level
    return jnp.minimum(jnp.maximum(result, -most), most).astype(kind)


def setup_inputs(seed: int = 0) -> dict:
    arg_keys = jax.random.split(jax.random.key(seed), 10)
    parent_field = centred(arg_keys[0], (LEV, NPX, NPY), 1.0, 6.0, ((1, 8), (2, 4)), jnp.float32)
    parent_sppt = jnp.clip(jax.random.uniform(arg_keys[1], (NPX, NPY), jnp.float32, -0.796875, 0.796875) * levels(arg_keys[1], (NPX, NPY), ((0, 8), (1, 4)), -0.4, 0.0), -0.796875, 0.796875).astype(jnp.bfloat16)
    child_storm = centred(arg_keys[2], (LEV, NCX, NCY), 1.0, 6.0, ((1, 8), (2, 4)), jnp.float32)
    child_sppt = jnp.clip(jax.random.uniform(arg_keys[3], (NCX, NCY), jnp.float32, -0.796875, 0.796875) * levels(arg_keys[3], (NCX, NCY), ((0, 8), (1, 4)), -0.4, 0.0), -0.796875, 0.796875).astype(jnp.bfloat16)
    wind = jnp.clip(jax.random.uniform(arg_keys[4], (2, LEV), jnp.float32, -0.3, 0.3), -0.3, 0.3)
    strip_dest_keys = jax.random.split(jax.random.fold_in(arg_keys[5], 1), (DEVICES * SLOTS) // SLOTS)
    strip_dest_turns = jax.random.permutation(jax.random.fold_in(arg_keys[5], 3), (DEVICES * SLOTS) // SLOTS)
    strip_dest = jax.vmap(lambda own, number: deal_out(jax.random.fold_in(arg_keys[5], 2), own, number, SLOTS, DEVICES, 1, CAP, 2))(strip_dest_keys, strip_dest_turns).reshape((DEVICES * SLOTS, 1))
    strip_row = touch_ends(jax.random.randint(arg_keys[6], (DEVICES * SLOTS,), 0, NRB), jax.random.fold_in(arg_keys[6], 1), 0, NRB - 1).astype(jnp.int32)
    strip_target = touch_ends(jax.random.randint(arg_keys[7], (DEVICES * SLOTS,), 0, CROWS), jax.random.fold_in(arg_keys[7], 1), 0, CROWS - 1).astype(jnp.int32)
    storm_shift = draw_storm_shift(jax.random.fold_in(arg_keys[9], 71), 0)
    return dict(parent_field=parent_field, parent_sppt=parent_sppt, child_storm=child_storm, child_sppt=child_sppt, wind=wind, strip_dest=strip_dest, strip_row=strip_row, strip_target=strip_target, storm_shift=storm_shift)


KAPPA = 0.1
VERTICAL = 0.1
NUDGE = 0.5


def refine_table(strip):
    coarse = jnp.arange(strip).astype(jnp.float32)
    finer = jnp.arange(3 * strip).astype(jnp.float32)
    position = jnp.clip((finer + 0.5) / 3.0 - 0.5, 0.0, strip - 1.0)
    return jnp.maximum(0.0, 1.0 - jnp.abs(position[None, :] - coarse[:, None]))


def tendency(padded, wind_x, wind_y):
    centre = padded[..., 1:-1, 1:-1]
    north = padded[..., 2:, 1:-1]
    south = padded[..., :-2, 1:-1]
    east = padded[..., 1:-1, 2:]
    west = padded[..., 1:-1, :-2]
    laplace = north + south + east + west - 4.0 * centre
    return KAPPA * laplace - wind_x * (0.5 * (north - south)) - wind_y * (0.5 * (east - west))


def vertical(field):
    upper = jnp.concatenate([field[1:], field[-1:]], axis=0)
    lower = jnp.concatenate([field[:1], field[:-1]], axis=0)
    return upper + lower - 2.0 * field


def reference(parent_field, parent_sppt, child_storm, child_sppt, wind, strip_dest, strip_row, strip_target, storm_shift):
    devices = N_GX * N_GY
    wind_x = wind[0][:, None, None]
    wind_y = wind[1][:, None, None]
    padded = jnp.pad(parent_field, ((0, 0), (1, 1), (1, 1)))
    new_parent = parent_field + (1.0 + parent_sppt.astype(jnp.float32)) * (
        tendency(padded, wind_x, wind_y) + VERTICAL * vertical(parent_field))

    def device_rows(field):
        blocks = field.reshape(LEV, N_GX, PBX, N_GY, PBY).transpose(1, 3, 0, 2, 4)
        return blocks.reshape(devices, LEV, NRB, STRIP)

    source = jnp.repeat(jnp.arange(devices, dtype=jnp.int32), SLOTS)
    old_values = device_rows(parent_field)[source, :, strip_row]
    new_values = device_rows(new_parent)[source, :, strip_row]
    total = devices * SLOTS
    data = jnp.stack([old_values, new_values], axis=1).reshape(total, 2 * LEV * STRIP)
    segment = (strip_dest[:, 0] * CROWS + strip_target).astype(jnp.int32)
    coarse = jax.ops.segment_sum(data, segment, num_segments=devices * CROWS)
    counts = jax.ops.segment_sum(jnp.ones((total,), jnp.float32), segment, num_segments=devices * CROWS)
    counts_grid = counts.reshape(N_GX, N_GY, CROWS).transpose(0, 2, 1).reshape(NCX, N_GY)
    counts_grid = jnp.repeat(counts_grid, CY, axis=1)
    coarse_levels = coarse.reshape(N_GX, N_GY, CROWS, 2, LEV, STRIP).transpose(4, 3, 0, 2, 1, 5)
    coarse_levels = coarse_levels.reshape(LEV, 2, NCX, N_GY, STRIP)

    blocks = child_storm.reshape(LEV, N_GX, NPIECE, PX, N_GY, CY)
    bands = []
    for piece in range(NPIECE):
        band = blocks[:, :, piece]
        band = jnp.roll(band, storm_shift[0, piece], axis=1)
        band = jnp.roll(band, storm_shift[1, piece], axis=3)
        bands.append(band)
    child_start = jnp.stack(bands, axis=2).reshape(LEV, NCX, NCY)

    table = refine_table(STRIP)
    factor = 1.0 + child_sppt.astype(jnp.float32)
    divisor = 1.0 + NUDGE * counts_grid

    def level_step(items):
        field, coarse_level, wind_pair = items
        boundary = jnp.einsum('axnd,de->axne', coarse_level, table,
                              precision=lax.Precision.HIGHEST).reshape(2, NCX, NCY)
        for substep in range(SUBSTEPS):
            padded_level = jnp.pad(field, 1)
            weight = (substep + 1) / 3.0
            target_value = boundary[0] + weight * (boundary[1] - boundary[0])
            field = (field + factor * tendency(padded_level, wind_pair[0], wind_pair[1])
                     + NUDGE * target_value) / divisor
        return field

    child = lax.map(level_step, (child_start, coarse_levels, wind.T))
    return new_parent, child
```

```python
import jax
import jax.numpy as jnp
from jax import lax
from jax.sharding import PartitionSpec as P

SUBSTEPS = 3
STRIP = 128
CAP = 2


KAPPA = 0.1
VERTICAL = 0.1
NUDGE = 0.5


def padded_2(block, sides, width):
    for axis, dim in sides:
        count = lax.axis_size(axis)
        forward = [(i, i + 1) for i in range(count - 1)]
        backward = [(target, source) for source, target in forward]
        low = lax.ppermute(
            lax.slice_in_dim(block, block.shape[dim] - width, None, axis=dim), axis, forward
        )
        high = lax.ppermute(lax.slice_in_dim(block, 0, width, axis=dim), axis, backward)
        block = jnp.concatenate([low, block, high], axis=dim)
    return block


def from_behind(value, axis, steps):
    count = lax.axis_size(axis)
    pairs = [(source, (source + steps) % count) for source in range(count)]
    return lax.ppermute(value, axis, pairs)


def refine_table(strip):
    coarse = jnp.arange(strip).astype(jnp.float32)
    finer = jnp.arange(3 * strip).astype(jnp.float32)
    position = jnp.clip((finer + 0.5) / 3.0 - 0.5, 0.0, strip - 1.0)
    return jnp.maximum(0.0, 1.0 - jnp.abs(position[None, :] - coarse[:, None]))


def tendency(padded, wind_x, wind_y):
    centre = padded[..., 1:-1, 1:-1]
    north = padded[..., 2:, 1:-1]
    south = padded[..., :-2, 1:-1]
    east = padded[..., 1:-1, 2:]
    west = padded[..., 1:-1, :-2]
    laplace = north + south + east + west - 4.0 * centre
    return KAPPA * laplace - wind_x * (0.5 * (north - south)) - wind_y * (0.5 * (east - west))


def vertical(field):
    upper = jnp.concatenate([field[1:], field[-1:]], axis=0)
    lower = jnp.concatenate([field[:1], field[:-1]], axis=0)
    return upper + lower - 2.0 * field


def shards(
    parent_field,
    parent_sppt,
    child_storm,
    child_sppt,
    wind,
    strip_dest,
    strip_row,
    strip_target,
    storm_shift,
):
    devices = lax.axis_size(("gx", "gy"))
    my_index = lax.axis_index(("gx", "gy"))
    wind_x = wind[0][:, None, None]
    wind_y = wind[1][:, None, None]
    padded = padded_2(parent_field, (("gx", 1), ("gy", 2)), 1)
    new_parent = parent_field + (1.0 + parent_sppt.astype(jnp.float32)) * (
        tendency(padded, wind_x, wind_y) + VERTICAL * vertical(parent_field)
    )
    levels, crows, widths = child_storm.shape
    npiece = storm_shift.shape[1]
    band_rows = crows // npiece
    col_count = lax.axis_size("gy")
    child = child_storm
    rows_count = lax.axis_size("gx")

    def mover(steps_x, steps_y):
        pairs = [
            (
                x * col_count + y,
                (x + steps_x) % rows_count * col_count + (y + steps_y) % col_count,
            )
            for x in range(rows_count)
            for y in range(col_count)
        ]
        if steps_x == 0 and steps_y == 0:
            return lambda band: band
        return lambda band: lax.ppermute(band, ("gx", "gy"), pairs)

    movers = [mover(x, y) for x in range(rows_count) for y in range(col_count)]
    which = storm_shift[0] * col_count + storm_shift[1]

    def route(_, item):
        band, place = item
        return None, lax.switch(place, movers, band)

    pieces = jnp.moveaxis(child.reshape(levels, npiece, band_rows, widths), 1, 0)
    _, bands = lax.scan(route, None, (pieces, which))
    child = jnp.moveaxis(bands, 0, 1).reshape(levels, crows, widths)
    dest_table = strip_dest.reshape(devices, -1)
    row_table = strip_row.reshape(devices, -1)
    target_table = strip_target.reshape(devices, -1)
    slots = dest_table.shape[1]
    my_dest = lax.dynamic_index_in_dim(dest_table, my_index, 0, keepdims=False)
    my_rows = lax.dynamic_index_in_dim(row_table, my_index, 0, keepdims=False)
    same_owner = my_dest[:, None] == my_dest[None, :]
    earlier = jnp.arange(slots)[None, :] < jnp.arange(slots)[:, None]
    rank = jnp.sum((same_owner & earlier).astype(jnp.int32), axis=1)
    slot_index = my_dest * CAP + rank
    send_select = (jnp.arange(devices * CAP)[:, None] == slot_index[None, :]).astype(jnp.float32)
    both_states = jnp.stack([parent_field, new_parent]).reshape(2, levels, -1, STRIP)
    strips = both_states.shape[2]
    row_hot = (my_rows[:, None] == jnp.arange(strips)[None, :]).astype(jnp.float32)
    select = jnp.dot(send_select, row_hot, preferred_element_type=jnp.float32)
    outgoing_strips = jnp.einsum(
        "sr,alrd->sald",
        select,
        both_states,
        precision=lax.Precision.HIGHEST,
        preferred_element_type=jnp.float32,
    ).reshape(devices * CAP, -1)
    incoming = lax.all_to_all(
        outgoing_strips, ("gx", "gy"), split_axis=0, concat_axis=0, tiled=True
    )
    mine = dest_table == my_index
    rank_all = jnp.sum((mine[:, None, :] & earlier[None]).astype(jnp.int32), axis=2)
    slot_ids = jnp.arange(CAP)
    hits = mine[:, None, :] & (rank_all[:, None, :] == slot_ids[None, :, None])
    chosen = jnp.sum(jnp.where(hits, target_table[:, None, :], 0), axis=2)
    target_rows = jnp.where(jnp.any(hits, axis=2), chosen, -1).reshape(-1)
    row_select = (jnp.arange(crows)[:, None] == target_rows[None, :]).astype(jnp.float32)
    coarse = jnp.dot(
        row_select, incoming, precision=lax.Precision.HIGHEST, preferred_element_type=jnp.float32
    )
    counts = jnp.sum(row_select, axis=1)
    boundary = jnp.einsum(
        "tald,de->alte",
        coarse.reshape(crows, 2, levels, STRIP),
        refine_table(STRIP),
        precision=lax.Precision.HIGHEST,
    )
    divisor = 1.0 + NUDGE * counts[None, :, None]
    factor = 1.0 + child_sppt.astype(jnp.float32)
    for substep in range(SUBSTEPS):
        padded_child = padded_2(child, (("gx", 1), ("gy", 2)), 1)
        weight = (substep + 1) / 3.0
        target_value = boundary[0] + weight * (boundary[1] - boundary[0])
        child = (
            child + factor * tendency(padded_child, wind_x, wind_y) + NUDGE * target_value
        ) / divisor
    return (new_parent, child)


def solution(mesh):
    placed = (
        P(None, "gx", "gy"),
        P("gx", "gy"),
        P(None, "gx", "gy"),
        P("gx", "gy"),
        P(),
        P(),
        P(),
        P(),
        P(),
    )
    return jax.shard_map(
        shards,
        mesh=mesh,
        in_specs=placed,
        out_specs=(P(None, "gx", "gy"), P(None, "gx", "gy")),
        check_vma=False,
    )
```

```python
import functools

import jax
import jax.numpy as jnp
from jax import lax
from jax.experimental import pallas as pl
from jax.experimental.pallas import tpu as pltpu
from jax.sharding import PartitionSpec as P

SUBSTEPS = 3
STRIP = 128
CAP = 2


KAPPA = 0.1
VERTICAL = 0.1
NUDGE = 0.5


def edges(low_edge, high_edge, axis):
    count = lax.axis_size(axis)
    forward = [(i, i + 1) for i in range(count - 1)]
    backward = [(target, source) for source, target in forward]
    return lax.ppermute(high_edge, axis, forward), lax.ppermute(low_edge, axis, backward)


def refine_table(strip):
    coarse = jnp.arange(strip).astype(jnp.float32)
    finer = jnp.arange(3 * strip).astype(jnp.float32)
    position = jnp.clip((finer + 0.5) / 3.0 - 0.5, 0.0, strip - 1.0)
    return jnp.maximum(0.0, 1.0 - jnp.abs(position[None, :] - coarse[:, None]))


def tendency(centre, wind_x, wind_y):
    below, above = edges(centre[:, 0], centre[:, -1], "gx")
    before, behind = edges(centre[:, :, 0], centre[:, :, -1], "gy")
    north = jnp.concatenate([centre[:, 1:], above[:, None]], axis=1)
    south = jnp.concatenate([below[:, None], centre[:, :-1]], axis=1)
    east = jnp.concatenate([centre[:, :, 1:], behind[:, :, None]], axis=2)
    west = jnp.concatenate([before[:, :, None], centre[:, :, :-1]], axis=2)
    laplace = north + south + east + west - 4.0 * centre
    return KAPPA * laplace - wind_x * (0.5 * (north - south)) - wind_y * (0.5 * (east - west))


def vertical(field):
    upper = jnp.concatenate([field[1:], field[-1:]], axis=0)
    lower = jnp.concatenate([field[:1], field[:-1]], axis=0)
    return upper + lower - 2.0 * field

LANES = 128
BLOCK = 4


def child_kernel(
    n_gx, n_gy, child_ref, bound_ref, factor_ref, inverse_ref, coef_ref, out_ref,
    first, second, sides, send_row, send_col, halo_row, halo_col, send_sem, recv_sem,
):
    rows, levels, width = child_ref.shape
    tall = LANES // levels
    ix, iy = lax.axis_index("gx"), lax.axis_index("gy")
    barrier = pltpu.get_barrier_semaphore()
    halo_row[...] = jnp.zeros_like(halo_row)
    halo_col[...] = jnp.zeros_like(halo_col)
    around = (
        (lax.rem(ix + n_gx - 1, n_gx), iy),
        (lax.rem(ix + 1, n_gx), iy),
        (ix, lax.rem(iy + n_gy - 1, n_gy)),
        (ix, lax.rem(iy + 1, n_gy)),
    )
    sends = (ix > 0, ix < n_gx - 1, iy > 0, iy < n_gy - 1)
    receives = (ix < n_gx - 1, ix > 0, iy < n_gy - 1, iy > 0)
    for place in around:
        pl.semaphore_signal(
            barrier, inc=1, device_id=place, device_id_type=pl.DeviceIdType.MESH
        )

    def copy_rows(b, _):
        first[pl.ds(1 + b * 8, 8)] = child_ref[pl.ds(b * 8, 8)]
        return 0

    lax.fori_loop(0, rows // 8, copy_rows, 0)
    lane = lax.broadcasted_iota(jnp.int32, (1, 1, LANES), 2)
    wide = lax.broadcasted_iota(jnp.int32, (1, 1, width), 2)
    high = lax.broadcasted_iota(jnp.int32, (LANES, LANES), 0) < LANES // 2
    spread = [jnp.concatenate([coef_ref[i]] * (width // LANES), axis=1)[None] for i in range(4)]

    def transfer(step, side):
        if side < 2:
            source, landing = send_row.at[step, side], halo_row.at[step, 1 - side]
        else:
            source, landing = send_col.at[step, side - 2], halo_col.at[step, 3 - side]
        return pltpu.make_async_remote_copy(
            src_ref=source,
            dst_ref=landing,
            send_sem=send_sem.at[step, side],
            recv_sem=recv_sem.at[step, side],
            device_id=around[side],
            device_id_type=pl.DeviceIdType.MESH,
        )

    for step in range(SUBSTEPS):
        now = (first, second)[step % 2]
        later = (second, first)[step % 2]
        send_row[step, 0] = now[1]
        send_row[step, 1] = now[rows]

        def pack(b, _, now=now, step=step):
            block = pl.ds(1 + b * tall, tall)
            left, right = now[block, :, 0:LANES], now[block, :, width - LANES : width]
            both = jnp.where(lane < LANES // 2, left, right).reshape(LANES, LANES).T
            send_col[step, 0, pl.ds(b, 1)] = both[0:1]
            send_col[step, 1, pl.ds(b, 1)] = both[LANES - 1 : LANES]
            return 0

        lax.fori_loop(0, rows // tall, pack, 0)
        if step == 0:
            pl.semaphore_wait(barrier, 4)
        for side in range(4):

            @pl.when(sends[side])
            def _(step=step, side=side):
                transfer(step, side).start()

        for side in range(4):

            @pl.when(receives[side])
            def _(step=step, side=side):
                transfer(step, side).wait_recv()

        now[0] = halo_row[step, 0]
        now[rows + 1] = halo_row[step, 1]

        def unpack(b, _, step=step):
            west = halo_col[step, 0, pl.ds(b, 1)]
            east = halo_col[step, 1, pl.ds(b, 1)]
            both = jnp.where(high, west, east).T
            sides[pl.ds(b * tall, tall)] = both.reshape(tall, levels, LANES)
            return 0

        lax.fori_loop(0, rows // tall, unpack, 0)
        weight = (step + 1) / 3.0

        def advance(b, _, step=step, now=now, later=later, weight=weight):
            row = b * BLOCK
            here = pl.ds(row, BLOCK)
            centre = now[pl.ds(row + 1, BLOCK)]
            south = now[here]
            north = now[pl.ds(row + 2, BLOCK)]
            edge = jnp.concatenate([sides[here]] * (width // LANES), axis=2)
            west = jnp.where(wide == 0, edge, pltpu.roll(centre, 1, 2))
            east = jnp.where(wide == width - 1, edge, pltpu.roll(centre, width - 1, 2))
            change = (
                spread[0] * north + spread[1] * south + spread[2] * east + spread[3] * west
                - 4.0 * KAPPA * centre
            )
            old, new = bound_ref[0, here], bound_ref[1, here]
            target = old + weight * (new - old)
            value = (centre + factor_ref[here] * change + NUDGE * target) * inverse_ref[here]
            if step == SUBSTEPS - 1:
                out_ref[here] = value
            else:
                later[pl.ds(row + 1, BLOCK)] = value
            return 0

        lax.fori_loop(0, rows // BLOCK, advance, 0)

    for step in range(SUBSTEPS):
        for side in range(4):

            @pl.when(sends[side])
            def _(step=step, side=side):
                transfer(step, side).wait_send()


def child_steps(child, bound, factor, inverse, coef):
    rows, levels, width = child.shape
    blocks = rows * levels // LANES
    return pl.pallas_call(
        functools.partial(child_kernel, lax.axis_size("gx"), lax.axis_size("gy")),
        out_shape=jax.ShapeDtypeStruct(child.shape, jnp.float32),
        in_specs=[pl.BlockSpec(memory_space=pltpu.VMEM)] * 5,
        out_specs=pl.BlockSpec(memory_space=pltpu.VMEM),
        scratch_shapes=[
            pltpu.VMEM((rows + 2, levels, width), jnp.float32),
            pltpu.VMEM((rows + 2, levels, width), jnp.float32),
            pltpu.VMEM((rows, levels, LANES), jnp.float32),
            pltpu.VMEM((SUBSTEPS, 2, levels, width), jnp.float32),
            pltpu.VMEM((SUBSTEPS, 2, blocks, LANES), jnp.float32),
            pltpu.VMEM((SUBSTEPS, 2, levels, width), jnp.float32),
            pltpu.VMEM((SUBSTEPS, 2, blocks, LANES), jnp.float32),
            pltpu.SemaphoreType.DMA((SUBSTEPS, 4)),
            pltpu.SemaphoreType.DMA((SUBSTEPS, 4)),
        ],
        compiler_params=pltpu.CompilerParams(
            collective_id=0, has_side_effects=True, vmem_limit_bytes=40 * 1024 * 1024
        ),
        cost_estimate=pl.CostEstimate(
            flops=60 * rows * levels * width,
            bytes_accessed=24 * rows * levels * width,
            transcendentals=0,
        ),
    )(child, bound, factor, inverse, coef)


def shards(
    parent_field,
    parent_sppt,
    child_storm,
    child_sppt,
    wind,
    strip_dest,
    strip_row,
    strip_target,
    storm_shift,
):
    devices = lax.axis_size(("gx", "gy"))
    my_index = lax.axis_index(("gx", "gy"))
    wind_x = wind[0][:, None, None]
    wind_y = wind[1][:, None, None]
    new_parent = parent_field + (1.0 + parent_sppt.astype(jnp.float32)) * (
        tendency(parent_field, wind_x, wind_y) + VERTICAL * vertical(parent_field)
    )
    levels, crows, widths = child_storm.shape
    npiece = storm_shift.shape[1]
    band_rows = crows // npiece
    col_count = lax.axis_size("gy")
    child = child_storm
    rows_count = lax.axis_size("gx")

    def mover(steps_x, steps_y):
        pairs = [
            (
                x * col_count + y,
                (x + steps_x) % rows_count * col_count + (y + steps_y) % col_count,
            )
            for x in range(rows_count)
            for y in range(col_count)
        ]
        if steps_x == 0 and steps_y == 0:
            return lambda band: band
        return lambda band: lax.ppermute(band, ("gx", "gy"), pairs)

    movers = [mover(x, y) for x in range(rows_count) for y in range(col_count)]
    which = storm_shift[0] * col_count + storm_shift[1]

    def route(_, item):
        band, place = item
        return None, lax.switch(place, movers, band)

    pieces = jnp.moveaxis(child, 0, 1).reshape(npiece, band_rows, levels, widths)
    _, bands = lax.scan(route, None, (pieces, which))
    child = bands.reshape(crows, levels, widths)
    dest_table = strip_dest.reshape(devices, -1)
    row_table = strip_row.reshape(devices, -1)
    target_table = strip_target.reshape(devices, -1)
    slots = dest_table.shape[1]
    my_dest = lax.dynamic_index_in_dim(dest_table, my_index, 0, keepdims=False)
    my_rows = lax.dynamic_index_in_dim(row_table, my_index, 0, keepdims=False)
    same_owner = my_dest[:, None] == my_dest[None, :]
    earlier = jnp.arange(slots)[None, :] < jnp.arange(slots)[:, None]
    rank = jnp.sum((same_owner & earlier).astype(jnp.int32), axis=1)
    slot_index = my_dest * CAP + rank
    send_select = (jnp.arange(devices * CAP)[:, None] == slot_index[None, :]).astype(jnp.float32)
    both_states = jnp.stack([parent_field, new_parent]).reshape(2, levels, -1, STRIP)
    strips = both_states.shape[2]
    row_hot = (my_rows[:, None] == jnp.arange(strips)[None, :]).astype(jnp.float32)
    select = jnp.dot(send_select, row_hot, preferred_element_type=jnp.float32)
    outgoing_strips = jnp.einsum(
        "sr,alrd->sald",
        select,
        both_states,
        precision=lax.Precision.HIGHEST,
        preferred_element_type=jnp.float32,
    ).reshape(devices * CAP, -1)
    incoming = lax.all_to_all(
        outgoing_strips, ("gx", "gy"), split_axis=0, concat_axis=0, tiled=True
    )
    mine = dest_table == my_index
    rank_all = jnp.sum((mine[:, None, :] & earlier[None]).astype(jnp.int32), axis=2)
    slot_ids = jnp.arange(CAP)
    hits = mine[:, None, :] & (rank_all[:, None, :] == slot_ids[None, :, None])
    chosen = jnp.sum(jnp.where(hits, target_table[:, None, :], 0), axis=2)
    target_rows = jnp.where(jnp.any(hits, axis=2), chosen, -1).reshape(-1)
    row_select = (jnp.arange(crows)[:, None] == target_rows[None, :]).astype(jnp.float32)
    coarse = jnp.dot(
        row_select, incoming, precision=lax.Precision.HIGHEST, preferred_element_type=jnp.float32
    )
    counts = jnp.sum(row_select, axis=1)
    boundary = jnp.einsum(
        "tald,de->atle",
        coarse.reshape(crows, 2, levels, STRIP),
        refine_table(STRIP),
        precision=lax.Precision.HIGHEST,
    )
    inverse = 1.0 / (1.0 + NUDGE * counts)
    inverse = jnp.broadcast_to(inverse[:, None, None], (crows, 1, widths))
    factor = (1.0 + child_sppt.astype(jnp.float32))[:, None, :]
    half_x, half_y = 0.5 * wind[0], 0.5 * wind[1]
    coef = jnp.stack([KAPPA - half_x, KAPPA + half_x, KAPPA - half_y, KAPPA + half_y])
    coef = jnp.broadcast_to(coef[:, :, None], (4, levels, LANES))
    child = jnp.moveaxis(child_steps(child, boundary, factor, inverse, coef), 1, 0)
    return (new_parent, child)


def solution(mesh):
    placed = (
        P(None, "gx", "gy"),
        P("gx", "gy"),
        P(None, "gx", "gy"),
        P("gx", "gy"),
        P(),
        P(),
        P(),
        P(),
        P(),
    )
    return jax.shard_map(
        shards,
        mesh=mesh,
        in_specs=placed,
        out_specs=(P(None, "gx", "gy"), P(None, "gx", "gy")),
        check_vma=False,
    )
```
